512 devices in a mesh: rows: 128 (over x_lo, y, z), grp: 4 (over x_hi, core).
Axes of the slice: x: 4 (x_hi: 2, x_lo: 2; x = x_hi * 2 + x_lo), y: 4, z: 16, core: 2. Of those that a mesh axis runs over, the one named last changes fastest.
Arguments:
- panel: float32 [524288, 1024], P(('rows', 'grp')), may hold values from -100 to 100
- sketch_matrix: float32 [1024, 128], replicated, may hold values from -0.1875 to 0.1875
Outputs:
- basis: float32 [524288, 128], P(('rows', 'grp'))
- projected: float32 [128, 1024], replicated
The draws below stay inside these ranges and needn't reach their ends.
All inputs are finite; a program needn't handle non-finite values.
Results may differ from the reference program's by a relative error of at most 0.000075.
Values sent between devices are 32-bit elements; how exact they have to be, the bound alone decides.
A program may use at most 64 MiB of HBM per device.

```python
import jax
import jax.numpy as jnp
from jax import lax

W = 1024
K = 128
ROWS = 524288


def draw_panel(key, part):
    key = jax.random.fold_in(key, 1)
    keys = jax.random.split(key, 5)
    position = jnp.arange(ROWS, dtype=jnp.float32) / jnp.float32(ROWS)
    column_scale = jnp.exp(jax.random.uniform(keys[0], (1, W), jnp.float32, -1.15, 1.15))
    row_rough = jnp.exp(jax.random.uniform(keys[1], (ROWS, 1), jnp.float32, -0.69, 0.69))
    shared_row = jnp.clip(jax.random.normal(keys[2], (ROWS, 1), jnp.float32), -4.0, 4.0)
    noise = jnp.clip(jax.random.normal(keys[3], (ROWS, W), jnp.float32), -6.0, 6.0)
    loading = jax.random.uniform(keys[4], (1, W), jnp.float32, -1.0, 1.0)
    trend = 0.5 + position
    row_scale = trend[:, None] * row_rough
    return row_scale * column_scale * (noise + loading * shared_row)


def gaussian(own_key, extent, width, limit, kind=jnp.bfloat16):
    values = width * jax.random.normal(own_key, extent, jnp.float32)
    return jnp.clip(values, min=-limit, max=limit).astype(kind)


def setup_inputs(seed: int = 0) -> dict:
    streams_of = jax.random.split(jax.random.key(seed), 3)
    panel = draw_panel(jax.random.fold_in(streams_of[2], 71), 0)
    sketch_matrix = gaussian(streams_of[1], (W, K), W ** -0.5, 0.1875, jnp.float32)
    return dict(panel=panel, sketch_matrix=sketch_matrix)


def reference(panel, sketch_matrix):
    precise = lax.Precision.HIGHEST
    sketch = jnp.dot(panel.astype(jnp.float32), sketch_matrix.astype(jnp.float32), precision=precise, preferred_element_type=jnp.float32)
    gram = jnp.dot(sketch.T.astype(jnp.float32), sketch.astype(jnp.float32), precision=precise, preferred_element_type=jnp.float32)
    lower_factor = jnp.linalg.cholesky(gram)
    identity = jnp.eye(K, dtype=lower_factor.dtype)
    inverse_lower = lax.linalg.triangular_solve(lower_factor, identity, left_side=True, lower=True)
    scaling = jnp.sqrt(jnp.float32(ROWS))
    basis = jnp.dot(sketch.astype(jnp.float32), inverse_lower.T.astype(jnp.float32), precision=precise, preferred_element_type=jnp.float32) * scaling
    projected = jnp.dot(basis.T.astype(jnp.float32), panel.astype(jnp.float32), precision=precise, preferred_element_type=jnp.float32) / jnp.float32(ROWS)
    return (basis, projected)
```

```python
import functools

import jax
import jax.numpy as jnp
from jax import lax
from jax.experimental import pallas as pl
from jax.experimental.pallas import tpu as pltpu
from jax.sharding import PartitionSpec as P

F32 = jnp.float32
BF16 = jnp.bfloat16
MESH = pl.DeviceIdType.MESH

W = 1024
K = 128
R = 1024
CHUNKS = 4
PLANE = 32
RING = 16
GRP = 4

TN = (((0,), (0,)), ((), ()))
NT = (((1,), (1,)), ((), ()))
NN = (((1,), (0,)), ((), ()))


def split(x):
    high = x.astype(BF16)
    return high, (x - high.astype(F32)).astype(BF16)


def dot(a, b, dims=NN):
    return lax.dot_general(a, b, dims, preferred_element_type=F32)


def inverse_factor(gram):
    n = len(gram)
    rows = list(gram)
    sub = lax.broadcasted_iota(jnp.int32, (8, K), 0)
    lane = lax.broadcasted_iota(jnp.int32, (8, K), 1)
    out = []
    for b in range(n):
        low = range(b + 1, n)
        column = {
            i: [jnp.broadcast_to(rows[i][:, 8 * b + j : 8 * b + j + 1], (8, K)) for j in range(8)] for i in range(b, n)
        }
        in_block = (lane >= 8 * b) & (lane < 8 * b + 8)
        block = jnp.where(in_block, (lane == sub + 8 * b).astype(F32), rows[b])
        rest = {i: jnp.where(in_block, 0.0, rows[i]) for i in low}
        own = column[b]
        pivots = jnp.ones((8, K), F32)
        for k in range(8):
            pivot = jnp.broadcast_to(own[k][k : k + 1, :], (8, K))
            pivots = jnp.where(sub == k, pivot, pivots)
            inverse = 1.0 / pivot
            ratio = {j: jnp.broadcast_to(own[j][k : k + 1, :], (8, K)) * inverse for j in range(k + 1, 8)}
            pivot_row = jnp.broadcast_to(block[k : k + 1, :], (8, K)) * inverse
            below = jnp.where(sub > k, own[k], 0.0)
            block = block - below * pivot_row
            for j in range(k + 1, 8):
                own[j] = own[j] - below * ratio[j]
            for i in low:
                factor = column[i][k]
                rest[i] = rest[i] - factor * pivot_row
                for j in range(k + 1, 8):
                    column[i][j] = column[i][j] - factor * ratio[j]
        for i in low:
            rows[i] = rest[i]
        out.append(jnp.where(lane <= sub + 8 * b, block, 0.0) * lax.rsqrt(pivots))
    return jnp.concatenate(out, 0)


def kernel(
    total,
    panel_hbm,
    matrix_hbm,
    basis_ref,
    projected_ref,
    panel,
    matrix,
    panel_high,
    panel_low,
    matrix_parts,
    sketch_parts,
    g_own,
    g_plane,
    g_ring,
    g_all,
    y_own,
    y_plane,
    y_ring,
    y_all,
    load_sem,
    sem,
):
    row, col = lax.axis_index("rows"), lax.axis_index("grp")
    z, xy = lax.rem(row, RING), lax.div(row, RING)
    q = xy * GRP + col

    def in_plane(step):
        t = lax.rem(q + step, PLANE)
        return t, (lax.div(t, GRP) * RING + z, lax.rem(t, GRP))

    def in_ring(step):
        t = lax.rem(z + step, RING)
        return t, (xy * RING + t, col)

    rows_each = R // CHUNKS
    loads = [
        pltpu.make_async_copy(
            panel_hbm.at[pl.ds(i * rows_each, rows_each)], panel.at[pl.ds(i * rows_each, rows_each)], load_sem.at[i]
        )
        for i in range(CHUNKS)
    ]
    load_matrix = pltpu.make_async_copy(matrix_hbm, matrix, load_sem.at[CHUNKS])
    load_matrix.start()
    for load in loads:
        load.start()

    barrier = pltpu.get_barrier_semaphore()
    for step in range(1, PLANE):
        pl.semaphore_signal(barrier, inc=1, device_id=in_plane(step)[1], device_id_type=MESH)
    for step in range(1, RING):
        pl.semaphore_signal(barrier, inc=1, device_id=in_ring(step)[1], device_id_type=MESH)

    def send(src, dst, phase, peer, count):
        for step in range(1, count):
            t, device = peer(step)
            pltpu.make_async_remote_copy(
                src(t), dst, sem.at[2 * phase], sem.at[2 * phase + 1], device_id=device, device_id_type=MESH
            ).start()

    def wait_sent(like, phase):
        pltpu.make_async_copy(like, like, sem.at[2 * phase]).wait()

    def wait_received(like, phase):
        pltpu.make_async_copy(like, like, sem.at[2 * phase + 1]).wait()

    load_matrix.wait()
    high, low = split(matrix[...])
    matrix_parts[:, :K] = high
    matrix_parts[:, K:] = low
    for i in range(CHUNKS):
        loads[i].wait()
        part = pl.ds(i * rows_each, rows_each)
        high, low = split(panel[part])
        panel_high[part] = high
        panel_low[part] = low
        both = dot(high, matrix_parts[...])
        sketch = both[:, :K] + both[:, K:] + dot(low, matrix_parts[:, :K])
        high, low = split(sketch)
        sketch_parts[part, :K] = high
        sketch_parts[part, K:] = low

    both = dot(sketch_parts[...], sketch_parts[...], TN)
    own_gram = (both[:K, :K] + both[K:, K:]) + (both[:K, K:] + both[K:, :K])
    for i in range(PLANE):
        g_own[i] = own_gram[4 * i : 4 * i + 4, :]
    pl.semaphore_wait(barrier, PLANE - 1 + RING - 1)
    g_plane[q] = g_own[q]
    send(lambda t: g_own.at[t], g_plane.at[q], 0, in_plane, PLANE)

    for c in range(2):
        cols = pl.ds(c * (W // 2), W // 2)
        both = dot(sketch_parts[...], panel_high[:, cols], TN)
        product = both[:K] + both[K:] + dot(sketch_parts[:, :K], panel_low[:, cols], TN)
        for i in range(16):
            y_own[16 * c + i] = product[8 * i : 8 * i + 8, :]
    y_plane[q] = y_own[q]
    send(lambda t: y_own.at[t], y_plane.at[q], 3, in_plane, PLANE)

    def added(ref, count):
        total_ = ref[0]
        for i in range(1, count):
            total_ = total_ + ref[i]
        return total_

    plane_rest, ring_rest = pl.ds(0, PLANE - 1), pl.ds(0, RING - 1)
    wait_received(g_plane.at[plane_rest], 0)
    g_ring[z] = added(g_plane, PLANE)
    send(lambda t: g_ring.at[z], g_ring.at[z], 1, in_ring, RING)

    wait_received(y_plane.at[plane_rest], 3)
    y_ring[z] = added(y_plane, PLANE)
    send(lambda t: y_ring.at[z], y_ring.at[z], 4, in_ring, RING)

    wait_received(g_ring.at[ring_rest], 1)
    g_all[q] = added(g_ring, RING)
    send(lambda t: g_all.at[q], g_all.at[q], 2, in_plane, PLANE)

    wait_received(g_all.at[plane_rest], 2)
    gram = [jnp.concatenate([g_all[2 * i], g_all[2 * i + 1]], 0) for i in range(16)]
    inverse_lower = inverse_factor(gram)

    scaling = jnp.sqrt(F32(total))
    high, low = split(inverse_lower * scaling)
    twice = jnp.concatenate([high, high], 1)
    basis_ref[...] = dot(sketch_parts[...], twice, NT) + dot(sketch_parts[:, :K], low, NT)

    wait_received(y_ring.at[ring_rest], 4)
    y_all[q] = added(y_ring, RING)
    send(lambda t: y_all.at[q], y_all.at[q], 5, in_plane, PLANE)

    wait_received(y_all.at[plane_rest], 5)
    for c in range(2):
        y_high, y_low = split(jnp.concatenate([y_all[16 * c + i] for i in range(16)], 0))
        product = dot(high, y_high) + (dot(low, y_high) + dot(high, y_low))
        projected_ref[:, c * (W // 2) : (c + 1) * (W // 2)] = product / F32(total)

    wait_sent(g_plane.at[plane_rest], 0)
    wait_sent(g_ring.at[ring_rest], 1)
    wait_sent(g_all.at[plane_rest], 2)
    wait_sent(y_plane.at[plane_rest], 3)
    wait_sent(y_ring.at[ring_rest], 4)
    wait_sent(y_all.at[plane_rest], 5)


def local(panel, sketch_matrix):
    total = R * PLANE * RING
    vmem = pl.BlockSpec(memory_space=pltpu.VMEM)
    hbm = pl.BlockSpec(memory_space=pltpu.HBM)
    return pl.pallas_call(
        functools.partial(kernel, total),
        out_shape=[jax.ShapeDtypeStruct((R, K), F32), jax.ShapeDtypeStruct((K, W), F32)],
        in_specs=[hbm, hbm],
        out_specs=[vmem, vmem],
        scratch_shapes=[
            pltpu.VMEM((R, W), F32),
            pltpu.VMEM((W, K), F32),
            pltpu.VMEM((R, W), BF16),
            pltpu.VMEM((R, W), BF16),
            pltpu.VMEM((W, 2 * K), BF16),
            pltpu.VMEM((R, 2 * K), BF16),
            pltpu.VMEM((PLANE, 4, K), F32),
            pltpu.VMEM((PLANE, 4, K), F32),
            pltpu.VMEM((RING, 4, K), F32),
            pltpu.VMEM((PLANE, 4, K), F32),
            pltpu.VMEM((PLANE, 8, W // 2), F32),
            pltpu.VMEM((PLANE, 8, W // 2), F32),
            pltpu.VMEM((RING, 8, W // 2), F32),
            pltpu.VMEM((PLANE, 8, W // 2), F32),
            pltpu.SemaphoreType.DMA((CHUNKS + 1,)),
            pltpu.SemaphoreType.DMA((12,)),
        ],
        compiler_params=pltpu.CompilerParams(
            vmem_limit_bytes=40 << 20, collective_id=0, has_side_effects=True
        ),
        cost_estimate=pl.CostEstimate(flops=600_000_000, bytes_accessed=6 << 20, transcendentals=0),
    )(panel, sketch_matrix)


def solution(mesh):
    return jax.shard_map(
        local,
        mesh=mesh,
        in_specs=(P(("rows", "grp"), None), P()),
        out_specs=(P(("rows", "grp"), None), P()),
        check_vma=False,
    )
```

```python
import functools

import jax
import jax.numpy as jnp
from jax import lax
from jax.experimental import pallas as pl
from jax.experimental.pallas import tpu as pltpu
from jax.sharding import PartitionSpec as P

F32 = jnp.float32
BF16 = jnp.bfloat16
MESH = pl.DeviceIdType.MESH

W = 1024
K = 128
R = 1024
CHUNKS = 4
PLANE = 32
RING = 16
GRP = 4
GRANT = 105 << 19
PARTS = 4
WIDE = W // 2 // PARTS
RING_ORDER = range(RING)

TN = (((0,), (0,)), ((), ()))
NT = (((1,), (1,)), ((), ()))
NN = (((1,), (0,)), ((), ()))


def split(x):
    high = x.astype(BF16)
    return high, (x - high.astype(F32)).astype(BF16)


def dot(a, b, dims=NN):
    return lax.dot_general(a, b, dims, preferred_element_type=F32)


def inverse_factor(gram):
    n = len(gram)
    rows = list(gram)
    sub = lax.broadcasted_iota(jnp.int32, (8, K), 0)
    lane = lax.broadcasted_iota(jnp.int32, (8, K), 1)
    out = []
    for b in range(n):
        low = range(b + 1, n)
        column = {
            i: [jnp.broadcast_to(rows[i][:, 8 * b + j : 8 * b + j + 1], (8, K)) for j in range(8)] for i in range(b, n)
        }
        in_block = (lane >= 8 * b) & (lane < 8 * b + 8)
        block = jnp.where(in_block, (lane == sub + 8 * b).astype(F32), rows[b])
        rest = {i: jnp.where(in_block, 0.0, rows[i]) for i in low}
        own = column[b]
        pivots = jnp.ones((8, K), F32)
        for k in range(8):
            pivot = jnp.broadcast_to(own[k][k : k + 1, :], (8, K))
            pivots = jnp.where(sub == k, pivot, pivots)
            inverse = 1.0 / pivot
            ratio = {j: jnp.broadcast_to(own[j][k : k + 1, :], (8, K)) * inverse for j in range(k + 1, 8)}
            pivot_row = jnp.broadcast_to(block[k : k + 1, :], (8, K)) * inverse
            below = jnp.where(sub > k, own[k], 0.0)
            block = block - below * pivot_row
            for j in range(k + 1, 8):
                own[j] = own[j] - below * ratio[j]
            for i in low:
                factor = column[i][k]
                rest[i] = rest[i] - factor * pivot_row
                for j in range(k + 1, 8):
                    column[i][j] = column[i][j] - factor * ratio[j]
        for i in low:
            rows[i] = rest[i]
        out.append(jnp.where(lane <= sub + 8 * b, block, 0.0) * lax.rsqrt(pivots))
    return jnp.concatenate(out, 0)


def kernel(
    total,
    panel_hbm,
    matrix_hbm,
    basis_ref,
    scaled_ref,
    y_all,
    panel,
    matrix,
    panel_high,
    panel_low,
    matrix_parts,
    sketch_parts,
    g_own,
    g_plane,
    g_ring,
    g_all,
    y_own,
    y_plane,
    y_ring,
    load_sem,
    sem,
    greeted,
):
    row, col = lax.axis_index("rows"), lax.axis_index("grp")
    z, xy = lax.rem(row, RING), lax.div(row, RING)
    q = xy * GRP + col

    def in_plane(step):
        t = lax.rem(q + step, PLANE)
        return t, (lax.div(t, GRP) * RING + z, lax.rem(t, GRP))

    def in_ring(t):
        return (xy * RING + t, col)

    rows_each = R // CHUNKS
    loads = [
        pltpu.make_async_copy(
            panel_hbm.at[pl.ds(i * rows_each, rows_each)], panel.at[pl.ds(i * rows_each, rows_each)], load_sem.at[i]
        )
        for i in range(CHUNKS)
    ]
    load_matrix = pltpu.make_async_copy(matrix_hbm, matrix, load_sem.at[CHUNKS])
    load_matrix.start()
    for load in loads:
        load.start()

    core = lax.rem(col, 2)
    half = col - core
    barrier = pltpu.get_barrier_semaphore()

    def greet(device):
        pl.semaphore_signal(barrier, inc=1, device_id=device, device_id_type=MESH)

    for i in range(PLANE // GRP):
        for j in range(GRP // 2):
            other = (lax.rem(xy + i, PLANE // GRP) * RING + z, lax.rem(half + 2 * j, GRP) + 1)
            if i or j:
                greet(other)
            else:

                @pl.when(core == 0)
                def _():
                    greet(other)

    for step in range(1, RING):
        greet((xy * RING + lax.rem(z + step, RING), half))

    def await_plane():
        @pl.when(core == 1)
        def _():
            pl.semaphore_wait(barrier, PLANE - 1)
            pl.semaphore_signal(greeted, inc=1, device_id=(row, half), device_id_type=MESH)

        @pl.when(core == 0)
        def _():
            pl.semaphore_wait(greeted, 1)

    def await_ring():
        @pl.when(core == 0)
        def _():
            pl.semaphore_wait(barrier, 2 * (RING - 1))
            pl.semaphore_signal(greeted, inc=1, device_id=(row, half + 1), device_id_type=MESH)

        @pl.when(core == 1)
        def _():
            pl.semaphore_wait(greeted, 1)

    def copy(src, dst, phase, device):
        pltpu.make_async_remote_copy(
            src, dst, sem.at[2 * phase], sem.at[2 * phase + 1], device_id=device, device_id_type=MESH
        ).start()

    def send_plane(src, dst, phase):
        for step in range(1, PLANE):
            t, device = in_plane(step)
            copy(src(t), dst, phase, device)

    def send_ring(src, phase):
        for t in RING_ORDER:

            @pl.when(t != z)
            def _():
                copy(src, src, phase, in_ring(t))

    def wait_sent(like, phase):
        pltpu.make_async_copy(like, like, sem.at[2 * phase]).wait()

    def wait_received(like, phase):
        pltpu.make_async_copy(like, like, sem.at[2 * phase + 1]).wait()

    load_matrix.wait()
    high, low = split(matrix[...])
    matrix_parts[:, :K] = high
    matrix_parts[:, K:] = low
    for i in range(CHUNKS):
        loads[i].wait()
        part = pl.ds(i * rows_each, rows_each)
        high, low = split(panel[part])
        panel_high[part] = high
        panel_low[part] = low
        both = dot(high, matrix_parts[...])
        rest = dot(low, matrix_parts[...])
        sketch = both[:, :K] + (both[:, K:] + rest[:, :K] + rest[:, K:])
        high, low = split(sketch)
        sketch_parts[part, :K] = high
        sketch_parts[part, K:] = low

    both = dot(sketch_parts[...], sketch_parts[...], TN)
    own_gram = (both[:K, :K] + both[K:, K:]) + (both[:K, K:] + both[K:, :K])
    for i in range(PLANE):
        g_own[i] = own_gram[4 * i : 4 * i + 4, :]
    for p in range(PARTS):
        for c in range(2):
            cols = pl.ds(c * (W // 2) + p * WIDE, WIDE)
            both = dot(sketch_parts[...], panel_high[:, cols], TN)
            rest = dot(sketch_parts[...], panel_low[:, cols], TN)
            product = both[:K] + (both[K:] + rest[:K] + rest[K:])
            for i in range(16):
                y_own[p, 16 * c + i] = product[8 * i : 8 * i + 8, :]
        y_plane[p, q] = y_own[p, q]
        if p == 0:
            g_plane[q] = g_own[q]
            await_plane()
            send_plane(lambda t: g_own.at[t], g_plane.at[q], 0)
        send_plane(lambda t: y_own.at[p, t], y_plane.at[p, q], 3 + 3 * p)

    def added(ref, count):
        sums = ref[0]
        for i in range(1, count):
            sums = sums + ref[i]
        return sums

    plane_rest, ring_rest = pl.ds(0, PLANE - 1), pl.ds(0, RING - 1)
    wait_received(g_plane.at[plane_rest], 0)
    g_ring[z] = added(g_plane, PLANE)
    await_ring()
    send_ring(g_ring.at[z], 1)

    for p in range(PARTS):
        wait_received(y_plane.at[p, plane_rest], 3 + 3 * p)
        y_ring[p, z] = added(y_plane.at[p], PLANE)
        send_ring(y_ring.at[p, z], 4 + 3 * p)

    wait_received(g_ring.at[ring_rest], 1)
    g_all[q] = added(g_ring, RING)
    send_plane(lambda t: g_all.at[q], g_all.at[q], 2)

    for p in range(PARTS):
        wait_received(y_ring.at[p, ring_rest], 4 + 3 * p)
        y_all[p, q] = added(y_ring.at[p], RING)
        send_plane(lambda t: y_all.at[p, q], y_all.at[p, q], 5 + 3 * p)

    wait_received(g_all.at[plane_rest], 2)
    gram = [jnp.concatenate([g_all[2 * i], g_all[2 * i + 1]], 0) for i in range(16)]
    inverse_lower = inverse_factor(gram)

    scaling = jnp.sqrt(F32(total))
    scaled = inverse_lower * scaling
    scaled_ref[...] = scaled
    high, low = split(scaled)
    twice = jnp.concatenate([high, high], 1)
    basis_ref[...] = dot(sketch_parts[...], twice, NT) + dot(sketch_parts[:, :K], low, NT)

    for p in range(PARTS):
        wait_received(y_all.at[p, plane_rest], 5 + 3 * p)

    wait_sent(g_plane.at[plane_rest], 0)
    wait_sent(g_ring.at[ring_rest], 1)
    wait_sent(g_all.at[plane_rest], 2)
    for p in range(PARTS):
        wait_sent(y_plane.at[p, plane_rest], 3 + 3 * p)
        wait_sent(y_ring.at[p, ring_rest], 4 + 3 * p)
        wait_sent(y_all.at[p, plane_rest], 5 + 3 * p)


def finish(total, basis_ref, scaled_ref, y_ref, basis_hbm, projected_hbm, projected, sem):
    pieces = 4
    rows_each = R // pieces
    writes = [
        pltpu.make_async_copy(
            basis_ref.at[pl.ds(i * rows_each, rows_each)], basis_hbm.at[pl.ds(i * rows_each, rows_each)], sem.at[i]
        )
        for i in range(pieces)
    ]
    for write in writes:
        write.start()
    high, low = split(scaled_ref[...])
    for p in range(PARTS):
        for c in range(2):
            y_high, y_low = split(jnp.concatenate([y_ref[p, 16 * c + i] for i in range(16)], 0))
            both = dot(jnp.concatenate([high, low], 0), y_high)
            rest = dot(jnp.concatenate([high, low], 0), y_low)
            product = both[:K] + (both[K:] + rest[:K] + rest[K:])
            cols = pl.ds(c * (W // 2) + p * WIDE, WIDE)
            projected[:, cols] = product * F32(1.0 / total)
            write = pltpu.make_async_copy(
                projected.at[:, cols], projected_hbm.at[:, cols], sem.at[pieces + 2 * p + c]
            )
            write.start()
            writes.append(write)
    for write in writes:
        write.wait()


def local(panel, sketch_matrix):
    total = R * PLANE * RING
    vmem = pl.BlockSpec(memory_space=pltpu.VMEM)
    hbm = pl.BlockSpec(memory_space=pltpu.HBM)
    basis, scaled, y = pl.pallas_call(
        functools.partial(kernel, total),
        out_shape=[
            jax.ShapeDtypeStruct((R, K), F32),
            jax.ShapeDtypeStruct((K, K), F32),
            jax.ShapeDtypeStruct((PARTS, PLANE, 8, WIDE), F32),
        ],
        in_specs=[hbm, hbm],
        out_specs=[vmem, vmem, vmem],
        scratch_shapes=[
            pltpu.VMEM((R, W), F32),
            pltpu.VMEM((W, K), F32),
            pltpu.VMEM((R, W), BF16),
            pltpu.VMEM((R, W), BF16),
            pltpu.VMEM((W, 2 * K), BF16),
            pltpu.VMEM((R, 2 * K), BF16),
            pltpu.VMEM((PLANE, 4, K), F32),
            pltpu.VMEM((PLANE, 4, K), F32),
            pltpu.VMEM((RING, 4, K), F32),
            pltpu.VMEM((PLANE, 4, K), F32),
            pltpu.VMEM((PARTS, PLANE, 8, WIDE), F32),
            pltpu.VMEM((PARTS, PLANE, 8, WIDE), F32),
            pltpu.VMEM((PARTS, RING, 8, WIDE), F32),
            pltpu.SemaphoreType.DMA((CHUNKS + 1,)),
            pltpu.SemaphoreType.DMA((6 + 6 * PARTS,)),
            pltpu.SemaphoreType.REGULAR,
        ],
        compiler_params=pltpu.CompilerParams(
            vmem_limit_bytes=GRANT, collective_id=0, has_side_effects=True
        ),
        cost_estimate=pl.CostEstimate(flops=600_000_000, bytes_accessed=6 << 20, transcendentals=0),
    )(panel, sketch_matrix)
    return pl.pallas_call(
        functools.partial(finish, total),
        out_shape=[jax.ShapeDtypeStruct((R, K), F32), jax.ShapeDtypeStruct((K, W), F32)],
        in_specs=[vmem, vmem, vmem],
        out_specs=[hbm, hbm],
        scratch_shapes=[pltpu.VMEM((K, W), F32), pltpu.SemaphoreType.DMA((4 + 2 * PARTS,))],
        compiler_params=pltpu.CompilerParams(vmem_limit_bytes=8 << 20),
    )(basis, scaled, y)


def solution(mesh):
    return jax.shard_map(
        local,
        mesh=mesh,
        in_specs=(P(("rows", "grp"), None), P()),
        out_specs=(P(("rows", "grp"), None), P()),
        check_vma=False,
    )
```

```python
import functools

import jax
import jax.numpy as jnp
from jax import lax
from jax.experimental import pallas as pl
from jax.experimental.pallas import tpu as pltpu
from jax.sharding import PartitionSpec as P

F32 = jnp.float32
BF16 = jnp.bfloat16
MESH = pl.DeviceIdType.MESH

W = 1024
K = 128
R = 1024
CHUNKS = 4
PLANE = 32
CHIPS = 16
RING = 16
GRP = 4
GRANT = 105 << 19
PARTS = 4
WIDE = W // 2 // PARTS
SIDE = 4
TURNS = [range(4), range(4, 7), range(7, RING)]
FAR_FIRST = sorted(
    [(dx, dy) for dx in range(SIDE) for dy in range(SIDE)],
    key=lambda d: -sum(min(o, SIDE - o) for o in d),
)

TN = (((0,), (0,)), ((), ()))
NT = (((1,), (1,)), ((), ()))
NN = (((1,), (0,)), ((), ()))


def split(x):
    high = x.astype(BF16)
    return high, (x - high.astype(F32)).astype(BF16)


def dot(a, b, dims=NN):
    return lax.dot_general(a, b, dims, preferred_element_type=F32)


def inverse_factor(gram):
    n = len(gram)
    rows = list(gram)
    sub = lax.broadcasted_iota(jnp.int32, (8, K), 0)
    lane = lax.broadcasted_iota(jnp.int32, (8, K), 1)
    out = []
    for b in range(n):
        low = range(b + 1, n)
        column = {
            i: [jnp.broadcast_to(rows[i][:, 8 * b + j : 8 * b + j + 1], (8, K)) for j in range(8)] for i in range(b, n)
        }
        in_block = (lane >= 8 * b) & (lane < 8 * b + 8)
        block = jnp.where(in_block, (lane == sub + 8 * b).astype(F32), rows[b])
        rest = {i: jnp.where(in_block, 0.0, rows[i]) for i in low}
        own = column[b]
        pivots = jnp.ones((8, K), F32)
        for k in range(8):
            pivot = jnp.broadcast_to(own[k][k : k + 1, :], (8, K))
            pivots = jnp.where(sub == k, pivot, pivots)
            inverse = 1.0 / pivot
            ratio = {j: jnp.broadcast_to(own[j][k : k + 1, :], (8, K)) * inverse for j in range(k + 1, 8)}
            pivot_row = jnp.broadcast_to(block[k : k + 1, :], (8, K)) * inverse
            below = jnp.where(sub > k, own[k], 0.0)
            block = block - below * pivot_row
            for j in range(k + 1, 8):
                own[j] = own[j] - below * ratio[j]
            for i in low:
                factor = column[i][k]
                rest[i] = rest[i] - factor * pivot_row
                for j in range(k + 1, 8):
                    column[i][j] = column[i][j] - factor * ratio[j]
        for i in low:
            rows[i] = rest[i]
        out.append(jnp.where(lane <= sub + 8 * b, block, 0.0) * lax.rsqrt(pivots))
    return jnp.concatenate(out, 0)


def kernel(
    total,
    panel_hbm,
    matrix_hbm,
    basis_ref,
    scaled_ref,
    y_all,
    panel,
    matrix,
    panel_high,
    panel_low,
    matrix_parts,
    sketch_parts,
    g_own,
    g_plane,
    g_ring,
    g_all,
    y_own,
    y_core,
    y_plane,
    y_ring,
    load_sem,
    sem,
    greeted,
):
    row, col = lax.axis_index("rows"), lax.axis_index("grp")
    z, xy = lax.rem(row, RING), lax.div(row, RING)
    q = xy * GRP + col

    core = lax.rem(col, 2)
    half = col - core
    y_at, x_at = lax.rem(xy, SIDE), lax.div(xy, SIDE) + half
    chip = xy * 2 + lax.div(col, 2)

    def in_plane(dx, dy, dc):
        x, y = lax.rem(x_at + dx, SIDE), lax.rem(y_at + dy, SIDE)
        xy_, grp = lax.rem(x, 2) * SIDE + y, lax.div(x, 2) * 2 + lax.rem(core + dc, 2)
        return xy_ * GRP + grp, xy_ * 2 + lax.div(x, 2), (xy_ * RING + z, grp)

    def in_ring(t):
        return (xy * RING + t, col)

    rows_each = R // CHUNKS
    loads = [
        pltpu.make_async_copy(
            panel_hbm.at[pl.ds(i * rows_each, rows_each)], panel.at[pl.ds(i * rows_each, rows_each)], load_sem.at[i]
        )
        for i in range(CHUNKS)
    ]
    load_matrix = pltpu.make_async_copy(matrix_hbm, matrix, load_sem.at[CHUNKS])
    load_matrix.start()
    for load in loads:
        load.start()

    barrier = pltpu.get_barrier_semaphore()

    def greet(device):
        pl.semaphore_signal(barrier, inc=1, device_id=device, device_id_type=MESH)

    for dx, dy in FAR_FIRST:
        row_, grp = in_plane(dx, dy, 0)[2]
        other = (row_, grp - core + 1)
        if dx or dy:
            greet(other)
        else:

            @pl.when(core == 0)
            def _():
                greet(other)

    for step in range(1, RING):
        greet((xy * RING + lax.rem(z + step, RING), half))

    def await_plane():
        @pl.when(core == 1)
        def _():
            pl.semaphore_wait(barrier, PLANE - 1)
            pl.semaphore_signal(greeted, inc=1, device_id=(row, half), device_id_type=MESH)

        @pl.when(core == 0)
        def _():
            pl.semaphore_wait(greeted, 1)

    def await_ring():
        @pl.when(core == 0)
        def _():
            pl.semaphore_wait(barrier, 2 * (RING - 1))
            pl.semaphore_signal(greeted, inc=1, device_id=(row, half + 1), device_id_type=MESH)

        @pl.when(core == 1)
        def _():
            pl.semaphore_wait(greeted, 1)

    def copy(src, dst, phase, device):
        pltpu.make_async_remote_copy(
            src, dst, sem.at[2 * phase], sem.at[2 * phase + 1], device_id=device, device_id_type=MESH
        ).start()

    def send_plane(src, dst, phase):
        for dx, dy in FAR_FIRST:
            for dc in range(2):
                if dx or dy or dc:
                    t, _, device = in_plane(dx, dy, dc)
                    copy(src(t), dst, phase, device)

    def send_ring(src, phase, planes):
        for t in planes:

            @pl.when(t != z)
            def _():
                copy(src, src, phase, in_ring(t))

    def wait_sent(like, phase):
        pltpu.make_async_copy(like, like, sem.at[2 * phase]).wait()

    def wait_received(like, phase):
        pltpu.make_async_copy(like, like, sem.at[2 * phase + 1]).wait()

    load_matrix.wait()
    high, low = split(matrix[...])
    matrix_parts[:, :K] = high
    matrix_parts[:, K:] = low
    for i in range(CHUNKS):
        loads[i].wait()
        part = pl.ds(i * rows_each, rows_each)
        high, low = split(panel[part])
        panel_high[part] = high
        panel_low[part] = low
        both = dot(high, matrix_parts[...])
        rest = dot(low, matrix_parts[...])
        sketch = both[:, :K] + (both[:, K:] + rest[:, :K] + rest[:, K:])
        high, low = split(sketch)
        sketch_parts[part, :K] = high
        sketch_parts[part, K:] = low

    both = dot(sketch_parts[...], sketch_parts[...], TN)
    own_gram = (both[:K, :K] + both[K:, K:]) + (both[:K, K:] + both[K:, :K])
    for i in range(PLANE):
        g_own[i] = own_gram[4 * i : 4 * i + 4, :]
    for p in range(PARTS):
        for c in range(2):
            cols = pl.ds(c * (W // 2) + p * WIDE, WIDE)
            both = dot(sketch_parts[...], panel_high[:, cols], TN)
            rest = dot(sketch_parts[...], panel_low[:, cols], TN)
            product = both[:K] + (both[K:] + rest[:K] + rest[K:])
            for i in range(CHIPS):
                y_own[p, c, i] = product[8 * i : 8 * i + 8, :]
        if p == 0:
            g_plane[q] = g_own[q]
            await_plane()
        copy(y_own.at[p, 1 - core], y_core.at[p], 6 + 4 * p, (row, half + 1 - core))
        if p == 0:
            send_plane(lambda t: g_own.at[t], g_plane.at[q], 0)
    for p in range(PARTS):
        wait_received(y_core.at[p], 6 + 4 * p)
        y_own[p, core] = y_own[p, core] + y_core[p]
        y_plane[p, chip] = y_own[p, core, chip]
        for dx, dy in FAR_FIRST[:-1]:
            _, t, device = in_plane(dx, dy, 0)
            copy(y_own.at[p, core, t], y_plane.at[p, chip], 3 + 4 * p, device)

    def added(ref, count):
        sums = ref[0]
        for i in range(1, count):
            sums = sums + ref[i]
        return sums

    place = core * CHIPS + chip
    plane_rest, ring_rest = pl.ds(0, PLANE - 1), pl.ds(0, RING - 1)
    wait_received(g_plane.at[plane_rest], 0)
    g_ring[z] = added(g_plane, PLANE)
    await_ring()
    send_ring(g_ring.at[z], 1, range(RING))

    for p in range(PARTS):
        wait_received(y_plane.at[p, pl.ds(0, CHIPS - 1)], 3 + 4 * p)
        y_ring[p, z] = added(y_plane.at[p], CHIPS)
        send_ring(y_ring.at[p, z], 4 + 4 * p, TURNS[0])
    for turn in TURNS[1:]:
        for p in range(PARTS):
            send_ring(y_ring.at[p, z], 4 + 4 * p, turn)

    wait_received(g_ring.at[ring_rest], 1)
    g_all[q] = added(g_ring, RING)
    send_plane(lambda t: g_all.at[q], g_all.at[q], 2)

    for p in range(PARTS):
        wait_received(y_ring.at[p, ring_rest], 4 + 4 * p)
        y_all[p, place] = added(y_ring.at[p], RING)
        send_plane(lambda t: y_all.at[p, place], y_all.at[p, place], 5 + 4 * p)

    wait_received(g_all.at[plane_rest], 2)
    gram = [jnp.concatenate([g_all[2 * i], g_all[2 * i + 1]], 0) for i in range(16)]
    inverse_lower = inverse_factor(gram)

    scaling = jnp.sqrt(F32(total))
    scaled = inverse_lower * scaling
    scaled_ref[...] = scaled
    high, low = split(scaled)
    twice = jnp.concatenate([high, high], 1)
    basis_ref[...] = dot(sketch_parts[...], twice, NT) + dot(sketch_parts[:, :K], low, NT)

    for p in range(PARTS):
        wait_received(y_all.at[p, plane_rest], 5 + 4 * p)

    wait_sent(g_plane.at[plane_rest], 0)
    wait_sent(g_ring.at[ring_rest], 1)
    wait_sent(g_all.at[plane_rest], 2)
    for p in range(PARTS):
        wait_sent(y_plane.at[p, pl.ds(0, CHIPS - 1)], 3 + 4 * p)
        wait_sent(y_core.at[p], 6 + 4 * p)
        wait_sent(y_ring.at[p, ring_rest], 4 + 4 * p)
        wait_sent(y_all.at[p, plane_rest], 5 + 4 * p)


def finish(total, basis_ref, scaled_ref, y_ref, basis_hbm, projected_hbm, projected, sem):
    pieces = 4
    rows_each = R // pieces
    writes = [
        pltpu.make_async_copy(
            basis_ref.at[pl.ds(i * rows_each, rows_each)], basis_hbm.at[pl.ds(i * rows_each, rows_each)], sem.at[i]
        )
        for i in range(pieces)
    ]
    for write in writes:
        write.start()
    high, low = split(scaled_ref[...])
    for p in range(PARTS):
        for c in range(2):
            y_high, y_low = split(jnp.concatenate([y_ref[p, 16 * c + i] for i in range(16)], 0))
            both = dot(jnp.concatenate([high, low], 0), y_high)
            rest = dot(jnp.concatenate([high, low], 0), y_low)
            product = both[:K] + (both[K:] + rest[:K] + rest[K:])
            cols = pl.ds(c * (W // 2) + p * WIDE, WIDE)
            projected[:, cols] = product * F32(1.0 / total)
            write = pltpu.make_async_copy(
                projected.at[:, cols], projected_hbm.at[:, cols], sem.at[pieces + 2 * p + c]
            )
            write.start()
            writes.append(write)
    for write in writes:
        write.wait()


def local(panel, sketch_matrix):
    total = R * PLANE * RING
    vmem = pl.BlockSpec(memory_space=pltpu.VMEM)
    hbm = pl.BlockSpec(memory_space=pltpu.HBM)
    basis, scaled, y = pl.pallas_call(
        functools.partial(kernel, total),
        out_shape=[
            jax.ShapeDtypeStruct((R, K), F32),
            jax.ShapeDtypeStruct((K, K), F32),
            jax.ShapeDtypeStruct((PARTS, PLANE, 8, WIDE), F32),
        ],
        in_specs=[hbm, hbm],
        out_specs=[vmem, vmem, vmem],
        scratch_shapes=[
            pltpu.VMEM((R, W), F32),
            pltpu.VMEM((W, K), F32),
            pltpu.VMEM((R, W), BF16),
            pltpu.VMEM((R, W), BF16),
            pltpu.VMEM((W, 2 * K), BF16),
            pltpu.VMEM((R, 2 * K), BF16),
            pltpu.VMEM((PLANE, 4, K), F32),
            pltpu.VMEM((PLANE, 4, K), F32),
            pltpu.VMEM((RING, 4, K), F32),
            pltpu.VMEM((PLANE, 4, K), F32),
            pltpu.VMEM((PARTS, 2, CHIPS, 8, WIDE), F32),
            pltpu.VMEM((PARTS, CHIPS, 8, WIDE), F32),
            pltpu.VMEM((PARTS, CHIPS, 8, WIDE), F32),
            pltpu.VMEM((PARTS, RING, 8, WIDE), F32),
            pltpu.SemaphoreType.DMA((CHUNKS + 1,)),
            pltpu.SemaphoreType.DMA((6 + 8 * PARTS,)),
            pltpu.SemaphoreType.REGULAR,
        ],
        compiler_params=pltpu.CompilerParams(
            vmem_limit_bytes=GRANT, collective_id=0, has_side_effects=True
        ),
        cost_estimate=pl.CostEstimate(flops=600_000_000, bytes_accessed=6 << 20, transcendentals=0),
    )(panel, sketch_matrix)
    return pl.pallas_call(
        functools.partial(finish, total),
        out_shape=[jax.ShapeDtypeStruct((R, K), F32), jax.ShapeDtypeStruct((K, W), F32)],
        in_specs=[vmem, vmem, vmem],
        out_specs=[hbm, hbm],
        scratch_shapes=[pltpu.VMEM((K, W), F32), pltpu.SemaphoreType.DMA((4 + 2 * PARTS,))],
        compiler_params=pltpu.CompilerParams(vmem_limit_bytes=8 << 20),
    )(basis, scaled, y)


def solution(mesh):
    return jax.shard_map(
        local,
        mesh=mesh,
        in_specs=(P(("rows", "grp"), None), P()),
        out_specs=(P(("rows", "grp"), None), P()),
        check_vma=False,
    )
```

```python
import functools

import jax
import jax.numpy as jnp
from jax import lax
from jax.experimental import pallas as pl
from jax.experimental.pallas import tpu as pltpu
from jax.sharding import PartitionSpec as P

F32 = jnp.float32
BF16 = jnp.bfloat16
MESH = pl.DeviceIdType.MESH

W = 1024
K = 128
R = 1024
CHUNKS = 4
PLANE = 32
CHIPS = 16
RING = 16
GRP = 4
GRANT = 105 << 19
PARTS = 4
WIDE = W // 2 // PARTS
SIDE = 4
TURNS = [range(4), range(4, 7), range(7, RING)]
FAR_FIRST = sorted(
    [(dx, dy) for dx in range(SIDE) for dy in range(SIDE)],
    key=lambda d: -sum(min(o, SIDE - o) for o in d),
)

TN = (((0,), (0,)), ((), ()))
NT = (((1,), (1,)), ((), ()))
NN = (((1,), (0,)), ((), ()))


def split(x):
    high = x.astype(BF16)
    return high, (x - high.astype(F32)).astype(BF16)


def dot(a, b, dims=NN):
    return lax.dot_general(a, b, dims, preferred_element_type=F32)


def inverse_factor(gram):
    n = len(gram)
    rows = list(gram)
    sub = lax.broadcasted_iota(jnp.int32, (8, K), 0)
    lane = lax.broadcasted_iota(jnp.int32, (8, K), 1)
    out = []
    for b in range(n):
        low = range(b + 1, n)
        column = {
            i: [jnp.broadcast_to(rows[i][:, 8 * b + j : 8 * b + j + 1], (8, K)) for j in range(8)] for i in range(b, n)
        }
        in_block = (lane >= 8 * b) & (lane < 8 * b + 8)
        block = jnp.where(in_block, (lane == sub + 8 * b).astype(F32), rows[b])
        rest = {i: jnp.where(in_block, 0.0, rows[i]) for i in low}
        own = column[b]
        pivots = jnp.ones((8, K), F32)
        for k in range(8):
            pivot = jnp.broadcast_to(own[k][k : k + 1, :], (8, K))
            pivots = jnp.where(sub == k, pivot, pivots)
            inverse = 1.0 / pivot
            ratio = {j: jnp.broadcast_to(own[j][k : k + 1, :], (8, K)) * inverse for j in range(k + 1, 8)}
            pivot_row = jnp.broadcast_to(block[k : k + 1, :], (8, K)) * inverse
            below = jnp.where(sub > k, own[k], 0.0)
            block = block - below * pivot_row
            for j in range(k + 1, 8):
                own[j] = own[j] - below * ratio[j]
            for i in low:
                factor = column[i][k]
                rest[i] = rest[i] - factor * pivot_row
                for j in range(k + 1, 8):
                    column[i][j] = column[i][j] - factor * ratio[j]
        for i in low:
            rows[i] = rest[i]
        out.append(jnp.where(lane <= sub + 8 * b, block, 0.0) * lax.rsqrt(pivots))
    return jnp.concatenate(out, 0)


def kernel(
    total,
    panel_hbm,
    matrix_hbm,
    basis_ref,
    scaled_ref,
    y_all,
    panel,
    matrix,
    panel_high,
    panel_low,
    matrix_parts,
    sketch_parts,
    g_own,
    g_plane,
    g_ring,
    g_all,
    y_own,
    y_core,
    y_plane,
    y_ring,
    load_sem,
    sem,
    greeted,
):
    row, col = lax.axis_index("rows"), lax.axis_index("grp")
    z, xy = lax.rem(row, RING), lax.div(row, RING)
    q = xy * GRP + col

    core = lax.rem(col, 2)
    half = col - core
    y_at, x_at = lax.rem(xy, SIDE), lax.div(xy, SIDE) + half
    chip = xy * 2 + lax.div(col, 2)

    def in_plane(dx, dy, dc):
        x, y = lax.rem(x_at + dx, SIDE), lax.rem(y_at + dy, SIDE)
        xy_, grp = lax.rem(x, 2) * SIDE + y, lax.div(x, 2) * 2 + lax.rem(core + dc, 2)
        return xy_ * GRP + grp, xy_ * 2 + lax.div(x, 2), (xy_ * RING + z, grp)

    def in_ring(t):
        return (xy * RING + t, col)

    rows_each = R // CHUNKS
    loads = [
        pltpu.make_async_copy(
            panel_hbm.at[pl.ds(i * rows_each, rows_each)], panel.at[pl.ds(i * rows_each, rows_each)], load_sem.at[i]
        )
        for i in range(CHUNKS)
    ]
    load_matrix = pltpu.make_async_copy(matrix_hbm, matrix, load_sem.at[CHUNKS])
    load_matrix.start()
    for load in loads:
        load.start()

    barrier = pltpu.get_barrier_semaphore()

    def greet(device):
        pl.semaphore_signal(barrier, inc=1, device_id=device, device_id_type=MESH)

    for dx, dy in FAR_FIRST:
        row_, grp = in_plane(dx, dy, 0)[2]
        other = (row_, grp - core + 1)
        if dx or dy:
            greet(other)
        else:

            @pl.when(core == 0)
            def _():
                greet(other)

    for step in range(1, RING):
        greet((xy * RING + lax.rem(z + step, RING), half))

    def await_plane():
        @pl.when(core == 1)
        def _():
            pl.semaphore_wait(barrier, PLANE - 1)
            pl.semaphore_signal(greeted, inc=1, device_id=(row, half), device_id_type=MESH)

        @pl.when(core == 0)
        def _():
            pl.semaphore_wait(greeted, 1)

    def await_ring():
        @pl.when(core == 0)
        def _():
            pl.semaphore_wait(barrier, 2 * (RING - 1))
            pl.semaphore_signal(greeted, inc=1, device_id=(row, half + 1), device_id_type=MESH)

        @pl.when(core == 1)
        def _():
            pl.semaphore_wait(greeted, 1)

    def copy(src, dst, phase, device):
        pltpu.make_async_remote_copy(
            src, dst, sem.at[2 * phase], sem.at[2 * phase + 1], device_id=device, device_id_type=MESH
        ).start()

    def send_plane(src, dst, phase):
        for dx, dy in FAR_FIRST:
            for dc in range(2):
                if dx or dy or dc:
                    t, _, device = in_plane(dx, dy, dc)
                    copy(src(t), dst, phase, device)

    def send_ring(src, phase, planes):
        for t in planes:

            @pl.when(t != z)
            def _():
                copy(src, src, phase, in_ring(t))

    def wait_sent(like, phase):
        pltpu.make_async_copy(like, like, sem.at[2 * phase]).wait()

    def wait_received(like, phase):
        pltpu.make_async_copy(like, like, sem.at[2 * phase + 1]).wait()

    load_matrix.wait()
    high, low = split(matrix[...])
    matrix_parts[:, :K] = high
    matrix_parts[:, K:] = low
    for i in range(CHUNKS):
        loads[i].wait()
        part = pl.ds(i * rows_each, rows_each)
        high, low = split(panel[part])
        panel_high[part] = high
        panel_low[part] = low
        both = dot(high, matrix_parts[...])
        rest = dot(low, matrix_parts[...])
        sketch = both[:, :K] + (both[:, K:] + rest[:, :K] + rest[:, K:])
        high, low = split(sketch)
        sketch_parts[part, :K] = high
        sketch_parts[part, K:] = low

    def multiply(p):
        for c in range(2):
            cols = pl.ds(c * (W // 2) + p * WIDE, WIDE)
            both = dot(sketch_parts[...], panel_high[:, cols], TN)
            rest = dot(sketch_parts[...], panel_low[:, cols], TN)
            product = both[:K] + (both[K:] + rest[:K] + rest[K:])
            for i in range(CHIPS):
                y_own[p, c, i] = product[8 * i : 8 * i + 8, :]
        if p == 0:
            await_plane()
        copy(y_own.at[p, 1 - core], y_core.at[p], 6 + 4 * p, (row, half + 1 - core))

    def exchange(p):
        wait_received(y_core.at[p], 6 + 4 * p)
        y_own[p, core] = y_own[p, core] + y_core[p]
        y_plane[p, chip] = y_own[p, core, chip]
        for dx, dy in FAR_FIRST[:-1]:
            _, t, device = in_plane(dx, dy, 0)
            copy(y_own.at[p, core, t], y_plane.at[p, chip], 3 + 4 * p, device)

    multiply(0)

    both = dot(sketch_parts[...], sketch_parts[...], TN)
    own_gram = (both[:K, :K] + both[K:, K:]) + (both[:K, K:] + both[K:, :K])
    for i in range(PLANE):
        g_own[i] = own_gram[4 * i : 4 * i + 4, :]
    g_plane[q] = g_own[q]
    send_plane(lambda t: g_own.at[t], g_plane.at[q], 0)

    for p in range(1, PARTS):
        multiply(p)
        exchange(p - 1)
    exchange(PARTS - 1)

    def added(ref, count):
        sums = ref[0]
        for i in range(1, count):
            sums = sums + ref[i]
        return sums

    place = core * CHIPS + chip
    plane_rest, ring_rest = pl.ds(0, PLANE - 1), pl.ds(0, RING - 1)
    wait_received(g_plane.at[plane_rest], 0)
    g_ring[z] = added(g_plane, PLANE)
    await_ring()
    send_ring(g_ring.at[z], 1, range(RING))

    for p in range(PARTS):
        wait_received(y_plane.at[p, pl.ds(0, CHIPS - 1)], 3 + 4 * p)
        y_ring[p, z] = added(y_plane.at[p], CHIPS)
        send_ring(y_ring.at[p, z], 4 + 4 * p, TURNS[0])
    for turn in TURNS[1:]:
        for p in range(PARTS):
            send_ring(y_ring.at[p, z], 4 + 4 * p, turn)

    wait_received(g_ring.at[ring_rest], 1)
    g_all[q] = added(g_ring, RING)
    send_plane(lambda t: g_all.at[q], g_all.at[q], 2)

    for p in range(PARTS):
        wait_received(y_ring.at[p, ring_rest], 4 + 4 * p)
        y_all[p, place] = added(y_ring.at[p], RING)
        send_plane(lambda t: y_all.at[p, place], y_all.at[p, place], 5 + 4 * p)

    wait_received(g_all.at[plane_rest], 2)
    gram = [jnp.concatenate([g_all[2 * i], g_all[2 * i + 1]], 0) for i in range(16)]
    inverse_lower = inverse_factor(gram)

    scaling = jnp.sqrt(F32(total))
    scaled = inverse_lower * scaling
    scaled_ref[...] = scaled
    high, low = split(scaled)
    twice = jnp.concatenate([high, high], 1)
    basis_ref[...] = dot(sketch_parts[...], twice, NT) + dot(sketch_parts[:, :K], low, NT)

    for p in range(PARTS):
        wait_received(y_all.at[p, plane_rest], 5 + 4 * p)

    wait_sent(g_plane.at[plane_rest], 0)
    wait_sent(g_ring.at[ring_rest], 1)
    wait_sent(g_all.at[plane_rest], 2)
    for p in range(PARTS):
        wait_sent(y_plane.at[p, pl.ds(0, CHIPS - 1)], 3 + 4 * p)
        wait_sent(y_core.at[p], 6 + 4 * p)
        wait_sent(y_ring.at[p, ring_rest], 4 + 4 * p)
        wait_sent(y_all.at[p, plane_rest], 5 + 4 * p)


def finish(total, basis_ref, scaled_ref, y_ref, basis_hbm, projected_hbm, projected, sem):
    pieces = 4
    rows_each = R // pieces
    writes = [
        pltpu.make_async_copy(
            basis_ref.at[pl.ds(i * rows_each, rows_each)], basis_hbm.at[pl.ds(i * rows_each, rows_each)], sem.at[i]
        )
        for i in range(pieces)
    ]
    for write in writes:
        write.start()
    high, low = split(scaled_ref[...])
    for p in range(PARTS):
        for c in range(2):
            y_high, y_low = split(jnp.concatenate([y_ref[p, 16 * c + i] for i in range(16)], 0))
            both = dot(jnp.concatenate([high, low], 0), y_high)
            rest = dot(jnp.concatenate([high, low], 0), y_low)
            product = both[:K] + (both[K:] + rest[:K] + rest[K:])
            cols = pl.ds(c * (W // 2) + p * WIDE, WIDE)
            projected[:, cols] = product * F32(1.0 / total)
            write = pltpu.make_async_copy(
                projected.at[:, cols], projected_hbm.at[:, cols], sem.at[pieces + 2 * p + c]
            )
            write.start()
            writes.append(write)
    for write in writes:
        write.wait()


def local(panel, sketch_matrix):
    total = R * PLANE * RING
    vmem = pl.BlockSpec(memory_space=pltpu.VMEM)
    hbm = pl.BlockSpec(memory_space=pltpu.HBM)
    basis, scaled, y = pl.pallas_call(
        functools.partial(kernel, total),
        out_shape=[
            jax.ShapeDtypeStruct((R, K), F32),
            jax.ShapeDtypeStruct((K, K), F32),
            jax.ShapeDtypeStruct((PARTS, PLANE, 8, WIDE), F32),
        ],
        in_specs=[hbm, hbm],
        out_specs=[vmem, vmem, vmem],
        scratch_shapes=[
            pltpu.VMEM((R, W), F32),
            pltpu.VMEM((W, K), F32),
            pltpu.VMEM((R, W), BF16),
            pltpu.VMEM((R, W), BF16),
            pltpu.VMEM((W, 2 * K), BF16),
            pltpu.VMEM((R, 2 * K), BF16),
            pltpu.VMEM((PLANE, 4, K), F32),
            pltpu.VMEM((PLANE, 4, K), F32),
            pltpu.VMEM((RING, 4, K), F32),
            pltpu.VMEM((PLANE, 4, K), F32),
            pltpu.VMEM((PARTS, 2, CHIPS, 8, WIDE), F32),
            pltpu.VMEM((PARTS, CHIPS, 8, WIDE), F32),
            pltpu.VMEM((PARTS, CHIPS, 8, WIDE), F32),
            pltpu.VMEM((PARTS, RING, 8, WIDE), F32),
            pltpu.SemaphoreType.DMA((CHUNKS + 1,)),
            pltpu.SemaphoreType.DMA((6 + 8 * PARTS,)),
            pltpu.SemaphoreType.REGULAR,
        ],
        compiler_params=pltpu.CompilerParams(
            vmem_limit_bytes=GRANT, collective_id=0, has_side_effects=True
        ),
        cost_estimate=pl.CostEstimate(flops=600_000_000, bytes_accessed=6 << 20, transcendentals=0),
    )(panel, sketch_matrix)
    return pl.pallas_call(
        functools.partial(finish, total),
        out_shape=[jax.ShapeDtypeStruct((R, K), F32), jax.ShapeDtypeStruct((K, W), F32)],
        in_specs=[vmem, vmem, vmem],
        out_specs=[hbm, hbm],
        scratch_shapes=[pltpu.VMEM((K, W), F32), pltpu.SemaphoreType.DMA((4 + 2 * PARTS,))],
        compiler_params=pltpu.CompilerParams(vmem_limit_bytes=8 << 20),
    )(basis, scaled, y)


def solution(mesh):
    return jax.shard_map(
        local,
        mesh=mesh,
        in_specs=(P(("rows", "grp"), None), P()),
        out_specs=(P(("rows", "grp"), None), P()),
        check_vma=False,
    )
```
